512 devices in a mesh: section: 8 (over x, y_hi), dp: 64 (over z, y_lo, core).
Axes of the slice: x: 4, y: 8 (y_hi: 2, y_lo: 4; y = y_hi * 4 + y_lo), z: 8, core: 2. Of those that a mesh axis runs over, the one named last changes fastest.
Arguments:
- stream_in: bfloat16 [8, 49344, 768], P('section', 'dp'), may hold values from -20 to 20
- timestep: int32 [192], P('dp'), may hold values from 0 to 999
- ln_gain: float32 [8, 768], P('section'), may hold values from 0.25 to 1.75
- qkv_weight: bfloat16 [8, 768, 2304], P('section', 'dp'), may hold values from -4 to 4
- out_weight: bfloat16 [8, 768, 768], P('section', 'dp'), may hold values from -0.75 to 0.75
- join_weight: bfloat16 [4, 1536, 768], P(None, 'dp'), may hold values from -0.15625 to 0.15625
- ctx_saved: bfloat16 [8, 49344, 768], P('section', 'dp'), may hold values from -16 to 16
- out_cot: bfloat16 [8, 49344, 768], P('section', 'dp'), may hold values from -0.02734375 to 0.02734375
Outputs:
- stream_out: bfloat16 [8, 49344, 768], P('section', 'dp')
- weight_grad: float32 [8, 768, 768], P('section', 'dp')
The draws below stay inside these ranges and needn't reach their ends.
All inputs are finite; a program needn't handle non-finite values.
Results may differ from the reference program's by a relative error of at most 0.013.
Values may be sent and summed in bfloat16 or wider, within the bound.
No kernel may reach another device: no remote copies, remote signals or barrier semaphores. Data moves between devices by JAX's collectives and lax.ppermute only.
A program may use at most 128 MiB of HBM per device.

```python
import math
import jax
import jax.numpy as jnp
from jax import lax

D = 768
HEADS = 12
HEAD_DIM = 64
SEQ = 257
IMAGES = 192
ROWS = 49344
N_SECTION = 8


def draw_qkv_weight(key, part):
    key = jax.random.fold_in(key, 11)
    first_key = jax.random.fold_in(key, 0)
    weight_scale = D ** (-0.5)
    full_shape = (N_SECTION, D, 3 * D)
    return (jax.random.normal(first_key, full_shape, jnp.float32) * weight_scale).astype(jnp.bfloat16)


def draw_stream_in(key, part):
    key = jax.random.fold_in(key, 23)
    first_key = jax.random.fold_in(key, 0)
    full_shape = (N_SECTION, ROWS, D)
    return jax.random.normal(first_key, full_shape, jnp.float32).astype(jnp.bfloat16)


def place_ends(entries, own_key, smallest, top_value):
    place = [jax.random.randint(jax.random.fold_in(own_key, axis), (), 0, length) for axis, length in enumerate(entries.shape)]
    widest = entries.shape.index(max(entries.shape))
    next_to = place[:widest] + [(place[widest] + 1) % entries.shape[widest]] + place[widest + 1:]
    return entries.at[tuple(place)].set(smallest).at[tuple(next_to)].set(top_value)


def with_spikes(values, own_key, source, target, shards_of, factor):
    def block_of(dim):
        return (jnp.arange(values.shape[dim]) // (values.shape[dim] // shards_of)).reshape((-1,) + (1,) * (values.ndim - 1 - dim))

    near = jax.random.permutation(own_key, shards_of)[block_of(target)]
    second = (block_of(target) + shards_of // 2) % shards_of
    return jnp.where((block_of(source) == near) | (block_of(source) == second), factor * values, values)


def block_scale(stream_key, shape, shards, smallest, largest):
    factor_of, own = 1.0, jax.random.fold_in(stream_key, 6)
    for axis_at, shards_of in shards:
        steps = jnp.exp(jax.random.uniform(jax.random.fold_in(own, axis_at), (shards_of,), jnp.float32, smallest / len(shards), largest / len(shards)))
        factor_of = factor_of * jnp.repeat(steps, shape[axis_at] // shards_of).reshape([-1 if axis == axis_at else 1 for axis in range(len(shape))])
    return factor_of


def noise(stream_key, shape, width, bound, cuts=(), kind=jnp.bfloat16):
    level = block_scale(stream_key, shape, cuts, -0.22, 0.18) if cuts else 1.0
    array = jax.random.normal(stream_key, shape, jnp.float32) * width * level
    return jnp.minimum(jnp.maximum(array, -bound), bound).astype(kind)


def bell_draw_with(rng, extent, width, limit, cuts, heavy, held_as=jnp.bfloat16):
    values = width * jax.random.normal(rng, extent, jnp.float32)
    if cuts:
        values = values * block_scale(rng, extent, cuts, -0.22, 0.18)
    return jnp.clip(with_spikes(values, jax.random.fold_in(rng, 3), *heavy), -limit, limit).astype(held_as)


def setup_inputs(seed: int = 0) -> dict:
    key_list = jax.random.split(jax.random.key(seed), 9)
    stream_in = draw_stream_in(jax.random.fold_in(key_list[8], 71), 0)
    timestep = place_ends(jax.random.randint(key_list[1], (IMAGES,), 0, 1000), jax.random.fold_in(key_list[1], 1), 0, 999).astype(jnp.int32)
    ln_gain = jnp.clip(1.0 + 0.15 * jax.random.normal(key_list[2], (N_SECTION, D), jnp.float32), 0.25, 1.75)
    qkv_weight = draw_qkv_weight(jax.random.fold_in(key_list[8], 71), 0)
    out_weight = noise(key_list[4], (N_SECTION, D, D), HEAD_DIM ** -0.5, 0.75, ((0, 8), (1, 64)))
    join_weight = noise(key_list[5], (N_SECTION // 2, 2 * D, D), (2 * D) ** -0.5, 0.15625, ((1, 64),))
    ctx_saved = bell_draw_with(key_list[6], (N_SECTION, ROWS, D), 1.0, 16.0, ((0, 8), (1, 64)), (1, 2, 64, 4.0))
    out_cot = noise(key_list[7], (N_SECTION, ROWS, D), ROWS ** -0.5, 0.02734375, ((0, 8), (1, 64)))
    return dict(stream_in=stream_in, timestep=timestep, ln_gain=ln_gain, qkv_weight=qkv_weight, out_weight=out_weight, join_weight=join_weight, ctx_saved=ctx_saved, out_cot=out_cot)


def time_rows(timestep):
    half_width = D // 2
    frequency = jnp.exp(-math.log(10000.0) * jnp.arange(half_width).astype(jnp.float32) / half_width)
    angles = timestep.astype(jnp.float32)[:, None] * frequency[None, :]
    return jnp.concatenate([jnp.cos(angles), jnp.sin(angles)], axis=1).astype(jnp.bfloat16)

def normalize(values, gain_row):
    floats = values.astype(jnp.float32)
    center = lax.optimization_barrier(jnp.mean(floats, axis=-1, keepdims=True))
    spread = lax.optimization_barrier(jnp.mean(jnp.square(floats - center), axis=-1, keepdims=True))
    return ((floats - center) * lax.rsqrt(spread + 1e-05) * gain_row.astype(jnp.float32)).astype(jnp.bfloat16)

def attend_image(qkv_rows):
    shaped = qkv_rows.reshape(SEQ, 3, HEADS, HEAD_DIM).astype(jnp.float32)
    queries = shaped[:, 0]
    key_rows = shaped[:, 1]
    value_rows = shaped[:, 2]
    scores = jnp.einsum('qhd,khd->hqk', queries, key_rows) * HEAD_DIM ** (-0.5)
    row_max = lax.optimization_barrier(jnp.max(scores, axis=-1, keepdims=True))
    powered = jnp.exp(scores - row_max)
    weights_soft = (powered / lax.optimization_barrier(jnp.sum(powered, axis=-1, keepdims=True))).astype(jnp.bfloat16)
    context = jnp.einsum('hqk,khd->qhd', weights_soft.astype(jnp.float32), value_rows)
    return context.astype(jnp.bfloat16).reshape(SEQ, D)

def section_block(block_in, gain_row, qkv_matrix, out_matrix):
    normed = normalize(block_in, gain_row)

    def one_image(rows_in):
        qkv_rows = jnp.dot(rows_in, qkv_matrix, preferred_element_type=jnp.float32).astype(jnp.bfloat16)
        return attend_image(qkv_rows)
    context = lax.map(one_image, normed.reshape(IMAGES, SEQ, D)).reshape(ROWS, D)
    projected = jnp.dot(context, out_matrix, preferred_element_type=jnp.float32)
    return (block_in.astype(jnp.float32) + projected).astype(jnp.bfloat16)

def reference(stream_in, timestep, ln_gain, qkv_weight, out_weight, join_weight, ctx_saved, out_cot):
    half_count = N_SECTION // 2
    time_token = time_rows(timestep)
    outputs = []
    grad_list = []
    for section_index in range(N_SECTION):
        entering = stream_in[section_index]
        if section_index == 0:
            entering = entering.reshape(IMAGES, SEQ, D).at[:, 0, :].set(time_token).reshape(ROWS, D)
        if section_index >= half_count:
            skip_in = stream_in[(N_SECTION - section_index) % N_SECTION]
            join_rows = join_weight[section_index - half_count]
            mixed_sum = jnp.dot(entering, join_rows[:D], preferred_element_type=jnp.float32)
            mixed_sum = mixed_sum + jnp.dot(skip_in, join_rows[D:], preferred_element_type=jnp.float32)
            block_in = mixed_sum.astype(jnp.bfloat16)
        else:
            block_in = entering
        outputs.append(section_block(block_in, ln_gain[section_index], qkv_weight[section_index], out_weight[section_index]))
        grad_list.append(jnp.dot(ctx_saved[section_index].T, out_cot[section_index], preferred_element_type=jnp.float32))
    stream_out = jnp.stack([outputs[(position - 1) % N_SECTION] for position in range(N_SECTION)])
    return (stream_out, jnp.stack(grad_list))
```

```python
import math

import jax
import jax.numpy as jnp
from jax import lax
from jax.experimental import pallas as pl
from jax.experimental.pallas import tpu as pltpu
from jax.sharding import Mesh
from jax.sharding import PartitionSpec as P

D = 768
HEADS = 12
HEAD_DIM = 64
SEQ = 257
PAD = 272
KEYS = 384
CUT = 112
SECTIONS = 8
REPLICAS = 64
AXES = ("x", "yh", "z", "yl", "c")
SECTION = ("x", "yh")


def time_rows(timestep):
    half_width = D // 2
    frequency = jnp.exp(
        -math.log(10000.0) * jnp.arange(half_width).astype(jnp.float32) / half_width
    )
    angles = timestep.astype(jnp.float32)[:, None] * frequency[None, :]
    return jnp.concatenate([jnp.cos(angles), jnp.sin(angles)], axis=1).astype(jnp.bfloat16)


def load_weights(place_ref, mine, other, w_qkv, w_out, w_join, sem):
    def copies(qkv_src, rest_src):
        made = []
        for z in range(8):
            rows = pl.ds(96 * z, 96)
            for part in range(3):
                made.append((qkv_src.at[z, pl.ds(96 * part, 96)], w_qkv.at[rows, pl.ds(D * part, D)]))
            made.append((rest_src.at[z, pl.ds(0, 96)], w_out.at[rows]))
            made.append((rest_src.at[z, pl.ds(96, 192)], w_join.at[pl.ds(192 * z, 192)]))
        return [pltpu.make_async_copy(s, d, sem.at[i]) for i, (s, d) in enumerate(made)]

    @pl.when(place_ref[0] == 0)
    def _():
        for copy in copies(mine, other):
            copy.start()

    @pl.when(place_ref[0] != 0)
    def _():
        for copy in copies(other, mine):
            copy.start()

    return copies(mine, other)


def block_kernel(
    images,
    first_image,
    pieces,
    place_ref,
    time_ref,
    gain_ref,
    mine,
    other,
    *refs,
):
    streams, skips, sides = (refs[i * len(pieces) : (i + 1) * len(pieces)] for i in range(3))
    out_ref, w_qkv, w_out, w_join, entering_rows, skip_rows, block_in, qkv_rows, context, sem = refs[
        3 * len(pieces) :
    ]
    section = place_ref[1]
    decoder = (section == 0) | (section >= 5)
    waits = load_weights(place_ref, mine, other, w_qkv, w_out, w_join, sem)
    qkv_rows[...] = jnp.zeros_like(qkv_rows)
    context[...] = jnp.zeros_like(context)
    for (image, start, count), stream, skip, side in zip(
        pieces, streams, skips, sides, strict=True
    ):
        rows = stream[...]
        if start == 0:
            first = lax.broadcasted_iota(jnp.int32, (count, D), 0) == 0
            token = time_ref[first_image + image].astype(jnp.bfloat16)
            rows = jnp.where(first & (section == 1), token, rows)
        entering_rows[image, start : start + count] = rows
        mirrored = jnp.where(section == 6, side[...], skip[...])
        skip_rows[image, start : start + count] = jnp.where(section == 5, rows, mirrored)
    for copy in waits:
        copy.wait()

    def one_image(image):
        entering = entering_rows[image]

        @pl.when(decoder)
        def _():
            mixed = jnp.dot(entering, w_join[:D], preferred_element_type=jnp.float32)
            mixed = mixed + jnp.dot(
                skip_rows[image], w_join[D:], preferred_element_type=jnp.float32
            )
            block_in[...] = mixed.astype(jnp.bfloat16)

        @pl.when(jnp.logical_not(decoder))
        def _():
            block_in[...] = entering

        floats = block_in[...].astype(jnp.float32)
        center = jnp.mean(floats, axis=-1, keepdims=True)
        moved = floats - center
        spread = jnp.mean(jnp.square(moved), axis=-1, keepdims=True)
        normed = (moved * lax.rsqrt(spread + 1e-05) * gain_ref[...]).astype(jnp.bfloat16)
        for part in range(3):
            columns = slice(D * part, D * part + D)
            qkv_rows[:SEQ, columns] = jnp.dot(
                normed, w_qkv[:, columns], preferred_element_type=jnp.float32
            ).astype(jnp.bfloat16)

        low_q = lax.broadcasted_iota(jnp.int32, (PAD, 128), 1) < HEAD_DIM
        low_k = lax.broadcasted_iota(jnp.int32, (KEYS, 128), 1) < HEAD_DIM
        real = lax.broadcasted_iota(jnp.int32, (PAD, 128), 1) == 0
        zero = jnp.zeros((), jnp.bfloat16)
        one = jnp.ones((), jnp.bfloat16)
        for pair in range(HEADS // 2):
            lanes = slice(128 * pair, 128 * pair + 128)
            queries = qkv_rows[:PAD, lanes]
            keys = qkv_rows[:, D + 128 * pair : D + 128 * pair + 128]
            values = qkv_rows[:, 2 * D + 128 * pair : 2 * D + 128 * pair + 128]
            sums = []
            for low in (True, False):
                here_q = low_q if low else jnp.logical_not(low_q)
                here_k = low_k if low else jnp.logical_not(low_k)
                scores = lax.dot_general(
                    jnp.where(here_q, queries, zero),
                    keys,
                    (((1,), (1,)), ((), ())),
                    preferred_element_type=jnp.float32,
                )
                main, last = scores[:, :256], jnp.where(real, scores[:, 256:], -1e30)
                row_max = jnp.maximum(
                    jnp.max(main, axis=-1, keepdims=True), jnp.max(last, axis=-1, keepdims=True)
                )
                factor = HEAD_DIM ** (-0.5) * math.log2(math.e)
                powered = jnp.concatenate(
                    [jnp.exp2((main - row_max) * factor), jnp.exp2((last - row_max) * factor)], axis=1
                ).astype(jnp.bfloat16)
                sums.append(
                    jnp.dot(powered, jnp.where(here_k, values, one), preferred_element_type=jnp.float32)
                )
            own = jnp.where(low_q, sums[0], sums[1])
            total = pltpu.roll(jnp.where(low_q, sums[1], sums[0]), HEAD_DIM, 1)
            context[:, lanes] = (own / total).astype(jnp.bfloat16)

        projected = jnp.dot(context[:SEQ], w_out[...], preferred_element_type=jnp.float32)
        out_ref[image] = (block_in[...].astype(jnp.float32) + projected).astype(jnp.bfloat16)

    if images == 1:
        one_image(0)
    else:
        pl.loop(0, images)(one_image)


def run_block(first_image, images, pieces, place, streams, skips, sides, times, gain_row, mine, other):
    whole = pl.BlockSpec(memory_space=pltpu.VMEM)
    there = pl.BlockSpec(memory_space=pl.ANY)

    def body(*refs):
        block_kernel(images, first_image, pieces, *refs)

    return pl.pallas_call(
        body,
        out_shape=jax.ShapeDtypeStruct((images, SEQ, D), jnp.bfloat16),
        in_specs=[pl.BlockSpec(memory_space=pltpu.SMEM), whole, whole, there, there]
        + [whole] * (3 * len(pieces)),
        out_specs=whole,
        scratch_shapes=[
            pltpu.VMEM((D, 3 * D), jnp.bfloat16),
            pltpu.VMEM((D, D), jnp.bfloat16),
            pltpu.VMEM((2 * D, D), jnp.bfloat16),
            pltpu.VMEM((images, SEQ, D), jnp.bfloat16),
            pltpu.VMEM((images, SEQ, D), jnp.bfloat16),
            pltpu.VMEM((SEQ, D), jnp.bfloat16),
            pltpu.VMEM((KEYS, 3 * D), jnp.bfloat16),
            pltpu.VMEM((PAD, D), jnp.bfloat16),
            pltpu.SemaphoreType.DMA((40,)),
        ],
        compiler_params=pltpu.CompilerParams(vmem_limit_bytes=40 * 2**20),
        cost_estimate=pl.CostEstimate(
            flops=images * 2 * SEQ * D * D * 7, bytes_accessed=8 * 2**20, transcendentals=0
        ),
    )(place, times, gain_row, mine, other, *streams, *skips, *sides)


def on_device(
    stream_in, timestep, ln_gain, qkv_weight, out_weight, join_weight, ctx_saved, out_cot
):
    section = lax.axis_index(SECTION)
    core = lax.axis_index("c")
    y_low = lax.axis_index("yl")
    place = jnp.stack([core, section]).astype(jnp.int32)
    onward = [(s, (s + 1) % SECTIONS) for s in range(SECTIONS)]
    swap = [(0, 1), (1, 0)]

    term = lax.dot_general(
        ctx_saved[0], out_cot[0], (((0,), (0,)), ((), ())), preferred_element_type=jnp.float32
    )
    left, right = term[:, : D // 2], term[:, D // 2 :]
    chip = jnp.where(core == 0, left, right) + lax.ppermute(
        jnp.where(core == 0, right, left), "c", swap
    )
    level = lax.psum_scatter(chip, "z", scatter_dimension=0, tiled=True)

    join_rows = lax.dynamic_index_in_dim(
        join_weight, jnp.clip(section - 4, 0, 3), 0, keepdims=False
    )
    for_low = qkv_weight[0].reshape(12, 3, D).transpose(1, 0, 2).reshape(36, D)
    for_high = jnp.concatenate([out_weight[0], join_rows], axis=0)
    straight = lax.ppermute(jnp.where(core == 0, for_low, for_high), SECTION, onward)
    crossed = lax.ppermute(
        jnp.where(core == 0, for_high, for_low),
        AXES,
        [
            (i, ((i // REPLICAS + 1) % SECTIONS) * REPLICAS + ((i % REPLICAS) ^ 1))
            for i in range(SECTIONS * REPLICAS)
        ],
    )
    pair = jnp.where(
        core == 0,
        jnp.concatenate([straight, crossed], axis=0),
        jnp.concatenate([crossed, straight], axis=0),
    )
    near = lax.all_gather(pair, "yl", axis=0, tiled=True)
    slot = lax.broadcasted_iota(jnp.int32, (288, 288), 0)
    source = lax.broadcasted_iota(jnp.int32, (288, 288), 1)
    from_qkv = (slot % 96) // 12 * 36 + slot // 96 * 12 + slot % 12
    rest = slot - 96
    from_rest = jnp.where(slot < 96, slot // 12 * 36 + slot % 12, rest // 24 * 36 + 12 + rest % 24)
    order = (source == jnp.where(core == 0, from_qkv, from_rest)).astype(jnp.bfloat16)
    near = jnp.dot(order, near, preferred_element_type=jnp.float32).astype(jnp.bfloat16)

    def onwards(part):
        return lax.ppermute(part, SECTION, onward), lax.ppermute(part, SECTION, [(1, 0), (2, 7)])

    def beside(part):
        return lax.ppermute(part, SECTION, [(3, 5)])

    def beside_on(part):
        return lax.ppermute(part, SECTION, [(5, 6)])

    image_0, image_1 = stream_in[0, :SEQ], stream_in[0, SEQ : 2 * SEQ]
    image_2 = stream_in[0, 2 * SEQ :]
    gain_row = lax.ppermute(ln_gain, SECTION, onward)
    stream_0, skip_0 = onwards(image_0)
    side_0 = beside_on(beside(image_0))
    side_1, side_2 = beside(image_1), beside(image_2)

    near, level, gain_row, stream_0, skip_0, side_0, side_1, side_2, image_1, image_2 = (
        lax.optimization_barrier(
            (near, level, gain_row, stream_0, skip_0, side_0, side_1, side_2, image_1, image_2)
        )
    )
    mine = lax.all_gather(near, "z", axis=0, tiled=False)
    stream_1, skip_1 = onwards(image_1)
    stream_2, skip_2 = onwards(image_2[:CUT])
    side_1, side_2 = beside_on(side_1), beside_on(side_2)

    level = level.reshape(4, 24, D // 2)
    total = lax.dynamic_index_in_dim(level, y_low, 0, keepdims=False)
    for step in range(1, 4):
        ring = [(i, (i + step) % 4) for i in range(4)]
        piece = lax.dynamic_index_in_dim(level, (y_low + step) % 4, 0, keepdims=False)
        total = total + lax.ppermute(piece, "yl", ring)
    low_rows, high_rows = total[:12], total[12:]
    own_half = jnp.where(core == 0, low_rows, high_rows)
    other_half = lax.ppermute(jnp.where(core == 0, high_rows, low_rows), "c", swap)
    weight_grad = jnp.where(
        core == 0,
        jnp.concatenate([own_half, other_half], axis=1),
        jnp.concatenate([other_half, own_half], axis=1),
    )

    (
        mine,
        weight_grad,
        stream_1,
        skip_1,
        side_1,
        stream_2,
        skip_2,
        side_2,
        image_2,
    ) = lax.optimization_barrier(
        (mine, weight_grad, stream_1, skip_1, side_1, stream_2, skip_2, side_2, image_2)
    )
    other = lax.ppermute(mine, "c", swap)
    stream_3, skip_3 = onwards(image_2[CUT:])

    times = time_rows(timestep).astype(jnp.float32).reshape(-1, 1, D)
    front_out = run_block(
        0,
        2,
        ((0, 0, SEQ), (1, 0, SEQ)),
        place,
        (stream_0, stream_1),
        (skip_0, skip_1),
        (side_0, side_1),
        times,
        gain_row,
        mine,
        other,
    )
    back_out = run_block(
        2,
        1,
        ((0, 0, CUT), (0, CUT, SEQ - CUT)),
        place,
        (stream_2, stream_3),
        (skip_2, skip_3),
        (side_2[:CUT], side_2[CUT:]),
        times,
        gain_row,
        mine,
        other,
    )
    stream_out = jnp.concatenate(
        [front_out.reshape(2 * SEQ, D), back_out.reshape(SEQ, D)], axis=0
    )
    return (stream_out[None], weight_grad[None])


def solution(mesh):
    fine = Mesh(mesh.devices.reshape(4, 2, 8, 4, 2), AXES)
    section, dp = ("x", "yh"), ("z", "yl", "c")
    return jax.shard_map(
        on_device,
        mesh=fine,
        in_specs=(
            P(section, dp, None),
            P(dp),
            P(section, None),
            P(section, dp, None),
            P(section, dp, None),
            P(None, dp, None),
            P(section, dp, None),
            P(section, dp, None),
        ),
        out_specs=(P(section, dp, None), P(section, dp, None)),
        check_vma=False,
    )
```

```python
import math

import jax
import jax.numpy as jnp
import numpy as np
from jax import lax
from jax.experimental import pallas as pl
from jax.experimental.pallas import tpu as pltpu
from jax.sharding import Mesh
from jax.sharding import PartitionSpec as P

D = 768
HEADS = 12
HEAD_DIM = 64
SEQ = 257
PAD = 272
KEYS = 384
HALF = D // 2
EARLY = 128
DIRECT = 384
SWAPS = 4
SECTIONS = 8
REPLICAS = 64
AXES = ("x", "yh", "z", "yl", "c")
SECTION = ("x", "yh")


def time_rows(timestep):
    half_width = D // 2
    frequency = jnp.exp(
        -math.log(10000.0) * jnp.arange(half_width).astype(jnp.float32) / half_width
    )
    angles = timestep.astype(jnp.float32)[:, None] * frequency[None, :]
    return jnp.concatenate([jnp.cos(angles), jnp.sin(angles)], axis=1).astype(jnp.bfloat16)


def gathered(mine, other, start, count):
    def rows(ref):
        return ref[:, start : start + count, :].reshape(-1, HALF)

    return jnp.concatenate(
        [rows(mine), jnp.concatenate([rows(ref) for ref in other], axis=0)], axis=1
    )


def block_kernel(place_ref, time_ref, gain_ref, mine, *refs):
    other, refs = refs[:SWAPS], refs[SWAPS:]
    early, late, direct, around, out_ref, *refs = refs
    entering_rows, skip_rows, out_rows, block_in, qkv_rows, context = refs
    images = entering_rows.shape[0]
    section = place_ref[1]
    decoder = (section == 0) | (section >= 5)
    first_half = pl.multiple_of(place_ref[0] * HALF, 128)
    second_half = pl.multiple_of(HALF - place_ref[0] * HALF, 128)
    natural = ((first_half, 0), (second_half, HALF))
    qkv_rows[...] = jnp.zeros_like(qkv_rows)
    context[...] = jnp.zeros_like(context)

    def assemble(rows, image, head, tail):
        start, stop = SEQ * image, SEQ * image + SEQ
        split = head.shape[0]
        cut = min(max(split, start), stop)
        if start < cut:
            rows[image, : cut - start] = head[start:cut]
        if cut < stop:
            rows[image, cut - start :] = tail[cut - split : stop - split]

    for image in range(images):
        assemble(entering_rows, image, early, late)

        @pl.when(section == 1)
        def _():
            entering_rows[image, :1] = time_ref[image].astype(jnp.bfloat16)

        @pl.when(section == 5)
        def _():
            skip_rows[image] = entering_rows[image]

        @pl.when(decoder & (section != 5))
        def _():
            assemble(skip_rows, image, direct, around)

    def one_image(image):
        entering = entering_rows[image]

        @pl.when(decoder)
        def _():
            join = gathered(mine, other, 4 * 96, 192)
            mixed = jnp.dot(entering, join[:D], preferred_element_type=jnp.float32)
            mixed = mixed + jnp.dot(
                skip_rows[image], join[D:], preferred_element_type=jnp.float32
            )
            for here, start in natural:
                block_in[:, pl.ds(here, HALF)] = mixed[:, start : start + HALF].astype(
                    jnp.bfloat16
                )

        @pl.when(jnp.logical_not(decoder))
        def _():
            block_in[...] = entering

        floats = block_in[...].astype(jnp.float32)
        center = jnp.mean(floats, axis=-1, keepdims=True)
        moved = floats - center
        spread = jnp.mean(jnp.square(moved), axis=-1, keepdims=True)
        normed = (moved * lax.rsqrt(spread + 1e-05) * gain_ref[...]).astype(jnp.bfloat16)
        for part in range(3):
            columns = slice(D * part, D * part + D)
            qkv_rows[:SEQ, columns] = jnp.dot(
                normed,
                gathered(mine, other, 96 * part, 96),
                preferred_element_type=jnp.float32,
            ).astype(jnp.bfloat16)

        low_q = lax.broadcasted_iota(jnp.int32, (PAD, 128), 1) < HEAD_DIM
        low_k = lax.broadcasted_iota(jnp.int32, (KEYS, 128), 1) < HEAD_DIM
        real = lax.broadcasted_iota(jnp.int32, (PAD, 128), 1) == 0
        zero = jnp.zeros((), jnp.bfloat16)
        one = jnp.ones((), jnp.bfloat16)
        for pair in range(HEADS // 2):
            lanes = slice(128 * pair, 128 * pair + 128)
            queries = qkv_rows[:PAD, lanes]
            keys = qkv_rows[:, D + 128 * pair : D + 128 * pair + 128]
            values = qkv_rows[:, 2 * D + 128 * pair : 2 * D + 128 * pair + 128]
            sums = []
            for low in (True, False):
                here_q = low_q if low else jnp.logical_not(low_q)
                here_k = low_k if low else jnp.logical_not(low_k)
                scores = lax.dot_general(
                    jnp.where(here_q, queries, zero),
                    keys,
                    (((1,), (1,)), ((), ())),
                    preferred_element_type=jnp.float32,
                )
                main, last = scores[:, :256], jnp.where(real, scores[:, 256:], -1e30)
                row_max = jnp.maximum(
                    jnp.max(main, axis=-1, keepdims=True), jnp.max(last, axis=-1, keepdims=True)
                )
                factor = HEAD_DIM ** (-0.5) * math.log2(math.e)
                powered = jnp.concatenate(
                    [jnp.exp2((main - row_max) * factor), jnp.exp2((last - row_max) * factor)], axis=1
                ).astype(jnp.bfloat16)
                sums.append(
                    jnp.dot(powered, jnp.where(here_k, values, one), preferred_element_type=jnp.float32)
                )
            own = jnp.where(low_q, sums[0], sums[1])
            total = pltpu.roll(jnp.where(low_q, sums[1], sums[0]), HEAD_DIM, 1)
            here, start = natural[pair // 3]
            column = pl.multiple_of(here + (128 * pair - start), 128)
            context[:, pl.ds(column, 128)] = (own / total).astype(jnp.bfloat16)

        projected = jnp.dot(
            context[:SEQ], gathered(mine, other, 3 * 96, 96), preferred_element_type=jnp.float32
        )
        for here, start in natural:
            columns = pl.ds(here, HALF)
            out_rows[image, :, columns] = (
                block_in[:, columns].astype(jnp.float32) + projected[:, start : start + HALF]
            ).astype(jnp.bfloat16)

    pl.loop(0, images)(one_image)
    for image in range(images):
        out_ref[SEQ * image : SEQ * image + SEQ] = out_rows[image]


def run_block(place, times, gain_row, mine, other, early, late, direct, around):
    whole = pl.BlockSpec(memory_space=pltpu.VMEM)
    rows = early.shape[0] + late.shape[0]
    images = rows // SEQ
    return pl.pallas_call(
        block_kernel,
        out_shape=jax.ShapeDtypeStruct((rows, D), jnp.bfloat16),
        in_specs=[pl.BlockSpec(memory_space=pltpu.SMEM)] + [whole] * (7 + SWAPS),
        out_specs=whole,
        scratch_shapes=[
            pltpu.VMEM((images, SEQ, D), jnp.bfloat16),
            pltpu.VMEM((images, SEQ, D), jnp.bfloat16),
            pltpu.VMEM((images, SEQ, D), jnp.bfloat16),
            pltpu.VMEM((SEQ, D), jnp.bfloat16),
            pltpu.VMEM((KEYS, 3 * D), jnp.bfloat16),
            pltpu.VMEM((PAD, D), jnp.bfloat16),
        ],
        compiler_params=pltpu.CompilerParams(vmem_limit_bytes=28 * 2**20),
        cost_estimate=pl.CostEstimate(
            flops=images * 2 * SEQ * D * D * 7, bytes_accessed=12 * 2**20, transcendentals=0
        ),
    )(place, times, gain_row, mine, *other, early, late, direct, around)


def arrival_places(core):
    slot = np.arange(576)
    deep = slot >= 384
    row = np.where(deep, slot - 384, slot % 96)
    depth = np.where(deep, 24, 12)
    arrival = (row // depth) % 2 ^ core
    packed = np.where(deep, 48, slot // 96 * 12) + row % depth
    return ((row // (2 * depth) * 2 + arrival) * 72 + packed).astype(np.int32)


def on_device(
    stream_in, timestep, ln_gain, qkv_weight, out_weight, join_weight, ctx_saved, out_cot
):
    section = lax.axis_index(SECTION)
    core = lax.axis_index("c")
    y_low = lax.axis_index("yl")
    place = jnp.stack([core, section]).astype(jnp.int32)
    onward = [(s, (s + 1) % SECTIONS) for s in range(SECTIONS)]
    swap = [(0, 1), (1, 0)]

    term = lax.dot_general(
        ctx_saved[0], out_cot[0], (((0,), (0,)), ((), ())), preferred_element_type=jnp.float32
    )
    level = lax.psum_scatter(term, "z", scatter_dimension=0, tiled=True)

    join_rows = lax.dynamic_index_in_dim(
        join_weight, jnp.clip(section - 4, 0, 3), 0, keepdims=False
    )

    def pack(half):
        columns = HALF * half
        qkv = lax.dynamic_slice_in_dim(qkv_weight[0].reshape(12, 3, D), columns, HALF, 2)
        return jnp.concatenate(
            [
                qkv.transpose(1, 0, 2).reshape(36, HALF),
                lax.dynamic_slice_in_dim(out_weight[0], columns, HALF, 1),
                lax.dynamic_slice_in_dim(join_rows, columns, HALF, 1),
            ],
            axis=0,
        )

    own_pack, cross_pack, whole = lax.optimization_barrier(
        (pack(core), pack(1 - core), stream_in[0])
    )
    straight = lax.ppermute(own_pack, SECTION, onward)
    crossed = lax.ppermute(
        cross_pack,
        AXES,
        [
            (i, ((i // REPLICAS + 1) % SECTIONS) * REPLICAS + ((i % REPLICAS) ^ 1))
            for i in range(SECTIONS * REPLICAS)
        ],
    )
    pair = jnp.concatenate([straight, crossed], axis=0)
    places = jnp.where(core == 0, arrival_places(0), arrival_places(1))
    source = lax.broadcasted_iota(jnp.int32, (576, 576), 1)
    order = (source == places[:, None]).astype(jnp.bfloat16)
    order, pair, gain = lax.optimization_barrier((order, pair, ln_gain))
    near = lax.all_gather(pair, "yl", axis=0, tiled=True)
    near = jnp.dot(
        order, near, preferred_element_type=jnp.float32
    ).astype(jnp.bfloat16)

    early = lax.ppermute(whole[:EARLY], SECTION, onward)
    gain_row = lax.ppermute(gain, SECTION, onward)
    moved = lax.ppermute(whole[DIRECT:], SECTION, [(1, 7), (2, 6), (3, 5)])

    near, whole, gain_row, moved, early = lax.optimization_barrier(
        (near, whole, gain_row, moved, early)
    )
    mine = lax.all_gather(near, "z", axis=0, tiled=False)
    late = lax.ppermute(whole[EARLY:], SECTION, onward)
    direct = lax.ppermute(whole[:DIRECT], SECTION, [(1, 0), (2, 7), (3, 6)])
    around = lax.ppermute(moved, SECTION, [(5, 6), (6, 7), (7, 0)])
    mine, direct, around = lax.optimization_barrier((mine, direct, around))
    other = [
        lax.ppermute(part, "c", swap) for part in jnp.split(mine, SWAPS, axis=0)
    ]

    times = time_rows(timestep).astype(jnp.float32).reshape(-1, 1, D)
    stream_out = run_block(place, times, gain_row, mine, other, early, late, direct, around)

    level = level.reshape(4, 2, 12, D)
    halves = [level[:, 0].reshape(48, D), level[:, 1].reshape(48, D)]
    level = jnp.where(core == 0, *halves) + lax.ppermute(
        jnp.where(core == 0, *halves[::-1]), "c", swap
    )
    level = level.reshape(4, 12, D)
    pieces = lax.all_to_all(level, "yl", 0, 0, tiled=True)
    stream_out, pieces = lax.optimization_barrier((stream_out, pieces))
    weight_grad = jnp.sum(pieces.reshape(4, 12, D), axis=0)
    return (stream_out[None], weight_grad[None])


def solution(mesh):
    fine = Mesh(mesh.devices.reshape(4, 2, 8, 4, 2), AXES)
    section, dp = ("x", "yh"), ("z", "yl", "c")
    return jax.shard_map(
        on_device,
        mesh=fine,
        in_specs=(
            P(section, dp, None),
            P(dp),
            P(section, None),
            P(section, dp, None),
            P(section, dp, None),
            P(None, dp, None),
            P(section, dp, None),
            P(section, dp, None),
        ),
        out_specs=(P(section, dp, None), P(section, dp, None)),
        check_vma=False,
    )
```

```python
import math

import jax
import jax.numpy as jnp
import numpy as np
from jax import lax
from jax.experimental import pallas as pl
from jax.experimental.pallas import tpu as pltpu
from jax.sharding import Mesh
from jax.sharding import PartitionSpec as P

D = 768
HEADS = 12
HEAD_DIM = 64
SEQ = 257
PAD = 272
KEYS = 384
HALF = D // 2
EARLY = 160
DIRECT = 384
SWAPS = 4
SECTIONS = 8
REPLICAS = 64
AXES = ("x", "yh", "z", "yl", "c")
SECTION = ("x", "yh")


def time_rows(timestep):
    half_width = D // 2
    frequency = jnp.exp(
        -math.log(10000.0) * jnp.arange(half_width).astype(jnp.float32) / half_width
    )
    angles = timestep.astype(jnp.float32)[:, None] * frequency[None, :]
    return jnp.concatenate([jnp.cos(angles), jnp.sin(angles)], axis=1).astype(jnp.bfloat16)


GROUPS = ((384, 192), (0, 288), (288, 96))


def weight_copies(mine, other, held, sems):
    copies = []
    for group, (start, count) in enumerate(GROUPS):
        rows = pl.ds(start, count)
        pairs = [(mine.at[:, rows], held.at[0, :, rows])]
        for i, ref in enumerate(other):
            deep = ref.shape[0]
            pairs.append((ref.at[:, rows], held.at[1, pl.ds(deep * i, deep), rows]))
        copies.append(
            [
                pltpu.make_async_copy(source, target, sems.at[group * len(pairs) + i])
                for i, (source, target) in enumerate(pairs)
            ]
        )
    return copies


def gathered(held, start, count):
    return jnp.concatenate(
        [held[half, :, start : start + count, :].reshape(-1, HALF) for half in range(2)], axis=1
    )


def block_kernel(place_ref, time_ref, gain_ref, mine, *refs):
    other, refs = refs[:SWAPS], refs[SWAPS:]
    early, late, direct, around, out_ref, *refs = refs
    held, entering, skip, block_in, normed, qkv_rows, image_context, context, sems = refs
    join_copies, qkv_copies, out_copies = weight_copies(mine, other, held, sems)
    for copy in join_copies + qkv_copies + out_copies:
        copy.start()
    count = out_ref.shape[0]
    images = count // SEQ
    section = place_ref[1]
    decoder = (section == 0) | (section >= 5)
    first_half = pl.multiple_of(place_ref[0] * HALF, 128)
    second_half = pl.multiple_of(HALF - place_ref[0] * HALF, 128)
    natural = ((first_half, 0), (second_half, HALF))
    for image in range(images):
        qkv_rows[image, 256:] = jnp.zeros((KEYS - 256, 3 * D), jnp.bfloat16)

    for copy in join_copies:
        copy.wait()

    @pl.when(decoder)
    def _():
        entering[:EARLY] = early[...]
        entering[EARLY:] = late[...]

        @pl.when(section == 5)
        def _():
            skip[...] = entering[...]

        @pl.when(section != 5)
        def _():
            skip[:DIRECT] = direct[...]
            skip[DIRECT:] = around[...]

        join = gathered(held, 4 * 96, 192)
        mixed = jnp.dot(entering[...], join[:D], preferred_element_type=jnp.float32)
        mixed = mixed + jnp.dot(skip[...], join[D:], preferred_element_type=jnp.float32)
        for here, start in natural:
            block_in[:count, pl.ds(here, HALF)] = mixed[:, start : start + HALF].astype(
                jnp.bfloat16
            )

    @pl.when(jnp.logical_not(decoder))
    def _():
        block_in[:EARLY] = early[...]
        block_in[EARLY:count] = late[...]

        @pl.when(section == 1)
        def _():
            for image in range(images):
                block_in[SEQ * image : SEQ * image + 1] = time_ref[image].astype(jnp.bfloat16)

    @pl.loop(0, block_in.shape[0] // 112)
    def _(part):
        rows = pl.ds(pl.multiple_of(part * 112, 16), 112)
        floats = block_in[rows].astype(jnp.float32)
        center = jnp.mean(floats, axis=-1, keepdims=True)
        moved = floats - center
        spread = jnp.mean(jnp.square(moved), axis=-1, keepdims=True)
        normed[rows] = (moved * lax.rsqrt(spread + 1e-05) * gain_ref[...]).astype(jnp.bfloat16)

    for copy in qkv_copies:
        copy.wait()
    for part in range(3):
        columns = slice(D * part, D * part + D)
        product = jnp.dot(
            normed[:count],
            gathered(held, 96 * part, 96),
            preferred_element_type=jnp.float32,
        ).astype(jnp.bfloat16)
        for image in range(images):
            qkv_rows[image, :SEQ, columns] = product[SEQ * image : SEQ * image + SEQ]

    @pl.loop(0, images)
    def _(image):
        low_q = lax.broadcasted_iota(jnp.int32, (PAD, 128), 1) < HEAD_DIM
        low_k = lax.broadcasted_iota(jnp.int32, (KEYS, 128), 1) < HEAD_DIM
        real = lax.broadcasted_iota(jnp.int32, (PAD, 128), 1) == 0
        zero = jnp.zeros((), jnp.bfloat16)
        one = jnp.ones((), jnp.bfloat16)
        for pair in range(HEADS // 2):
            lanes = 128 * pair
            queries = qkv_rows[image, :PAD, lanes : lanes + 128]
            keys = qkv_rows[image, :, D + lanes : D + lanes + 128]
            values = qkv_rows[image, :, 2 * D + lanes : 2 * D + lanes + 128]
            sums = []
            for low in (True, False):
                here_q = low_q if low else jnp.logical_not(low_q)
                here_k = low_k if low else jnp.logical_not(low_k)
                scores = lax.dot_general(
                    jnp.where(here_q, queries, zero),
                    keys,
                    (((1,), (1,)), ((), ())),
                    preferred_element_type=jnp.float32,
                )
                main, last = scores[:, :256], jnp.where(real, scores[:, 256:], -1e30)
                widest = jnp.maximum(jnp.maximum(main[:, :128], main[:, 128:]), last)
                row_max = jnp.max(widest, axis=-1, keepdims=True)
                factor = HEAD_DIM ** (-0.5) * math.log2(math.e)
                powered = jnp.concatenate(
                    [jnp.exp2((main - row_max) * factor), jnp.exp2((last - row_max) * factor)], axis=1
                ).astype(jnp.bfloat16)
                sums.append(
                    jnp.dot(powered, jnp.where(here_k, values, one), preferred_element_type=jnp.float32)
                )
            own = jnp.where(low_q, sums[0], sums[1])
            total = pltpu.roll(jnp.where(low_q, sums[1], sums[0]), HEAD_DIM, 1)
            here, start = natural[pair // 3]
            column = pl.multiple_of(here + (lanes - start), 128)
            image_context[image, :, pl.ds(column, 128)] = (own / total).astype(jnp.bfloat16)

    for image in range(images):
        context[SEQ * image : SEQ * image + SEQ] = image_context[image, :SEQ]
    for copy in out_copies:
        copy.wait()
    projected = jnp.dot(
        context[...], gathered(held, 3 * 96, 96), preferred_element_type=jnp.float32
    )
    for here, start in natural:
        columns = pl.ds(here, HALF)
        out_ref[:, columns] = (
            block_in[:count, columns].astype(jnp.float32) + projected[:, start : start + HALF]
        ).astype(jnp.bfloat16)


def run_block(place, times, gain_row, mine, other, early, late, direct, around):
    whole = pl.BlockSpec(memory_space=pltpu.VMEM)
    rows = early.shape[0] + late.shape[0]
    images = rows // SEQ
    return pl.pallas_call(
        block_kernel,
        out_shape=jax.ShapeDtypeStruct((rows, D), jnp.bfloat16),
        in_specs=[pl.BlockSpec(memory_space=pltpu.SMEM)]
        + [whole] * 2
        + [pl.BlockSpec(memory_space=pl.ANY)] * (1 + SWAPS)
        + [whole] * 4,
        out_specs=whole,
        scratch_shapes=[
            pltpu.VMEM((2, *mine.shape), jnp.bfloat16),
            pltpu.VMEM((rows, D), jnp.bfloat16),
            pltpu.VMEM((rows, D), jnp.bfloat16),
            pltpu.VMEM((pl.cdiv(rows, 112) * 112, D), jnp.bfloat16),
            pltpu.VMEM((pl.cdiv(rows, 112) * 112, D), jnp.bfloat16),
            pltpu.VMEM((images, KEYS, 3 * D), jnp.bfloat16),
            pltpu.VMEM((images, PAD, D), jnp.bfloat16),
            pltpu.VMEM((rows, D), jnp.bfloat16),
            pltpu.SemaphoreType.DMA((len(GROUPS) * (1 + SWAPS),)),
        ],
        compiler_params=pltpu.CompilerParams(vmem_limit_bytes=57 * 2**20),
        cost_estimate=pl.CostEstimate(
            flops=images * 2 * SEQ * D * D * 7, bytes_accessed=12 * 2**20, transcendentals=0
        ),
    )(place, times, gain_row, mine, *other, early, late, direct, around)


def arrival_places(core):
    slot = np.arange(576)
    deep = slot >= 384
    row = np.where(deep, slot - 384, slot % 96)
    depth = np.where(deep, 24, 12)
    arrival = (row // depth) % 2 ^ core
    packed = np.where(deep, 48, slot // 96 * 12) + row % depth
    return ((row // (2 * depth) * 2 + arrival) * 72 + packed).astype(np.int32)


def on_device(
    stream_in, timestep, ln_gain, qkv_weight, out_weight, join_weight, ctx_saved, out_cot
):
    section = lax.axis_index(SECTION)
    core = lax.axis_index("c")
    y_low = lax.axis_index("yl")
    place = jnp.stack([core, section]).astype(jnp.int32)
    onward = [(s, (s + 1) % SECTIONS) for s in range(SECTIONS)]
    swap = [(0, 1), (1, 0)]

    term = lax.dot_general(
        ctx_saved[0], out_cot[0], (((0,), (0,)), ((), ())), preferred_element_type=jnp.float32
    )
    level = lax.psum_scatter(term, "z", scatter_dimension=0, tiled=True)

    join_rows = lax.dynamic_index_in_dim(
        join_weight, jnp.clip(section - 4, 0, 3), 0, keepdims=False
    )

    high = lax.reduce_precision(ln_gain, 8, 7)
    middle = lax.reduce_precision(ln_gain - high, 8, 7)
    gain_parts = jnp.concatenate([high, middle, ln_gain - high - middle], axis=0).astype(
        jnp.bfloat16
    )

    def pack(half, gain_half):
        columns = HALF * half
        qkv = lax.dynamic_slice_in_dim(qkv_weight[0].reshape(12, 3, D), columns, HALF, 2)
        return jnp.concatenate(
            [
                qkv.transpose(1, 0, 2).reshape(36, HALF),
                lax.dynamic_slice_in_dim(out_weight[0], columns, HALF, 1),
                lax.dynamic_slice_in_dim(join_rows, columns, HALF, 1),
                lax.dynamic_slice_in_dim(gain_parts, HALF * gain_half, HALF, 1),
            ],
            axis=0,
        )

    own_pack, cross_pack, whole = lax.optimization_barrier(
        (pack(core, core), pack(1 - core, core), stream_in[0])
    )
    straight = lax.ppermute(own_pack, SECTION, onward)
    crossed = lax.ppermute(
        cross_pack,
        AXES,
        [
            (i, ((i // REPLICAS + 1) % SECTIONS) * REPLICAS + ((i % REPLICAS) ^ 1))
            for i in range(SECTIONS * REPLICAS)
        ],
    )
    gain_halves = [
        jnp.sum(part[72:].astype(jnp.float32), axis=0, keepdims=True) for part in (straight, crossed)
    ]
    gain_row = jnp.where(
        core == 0,
        jnp.concatenate(gain_halves, axis=1),
        jnp.concatenate(gain_halves[::-1], axis=1),
    )
    pair = jnp.concatenate([straight[:72], crossed[:72]], axis=0)
    places = jnp.where(core == 0, arrival_places(0), arrival_places(1))
    source = lax.broadcasted_iota(jnp.int32, (576, 576), 1)
    order = (source == places[:, None]).astype(jnp.bfloat16)
    order, pair = lax.optimization_barrier((order, pair))
    near = lax.all_gather(pair, "yl", axis=0, tiled=True)
    near = jnp.dot(
        order, near, preferred_element_type=jnp.float32
    ).astype(jnp.bfloat16)

    early = lax.ppermute(whole[:EARLY], SECTION, onward)
    moved = lax.ppermute(whole[DIRECT:], SECTION, [(1, 7), (2, 6), (3, 5)])

    near, part_direct, part_late, gain_row, moved, early = lax.optimization_barrier(
        (near, whole[:DIRECT], whole[EARLY:], gain_row, moved, early)
    )
    mine = lax.all_gather(near, "z", axis=0, tiled=False)
    late = lax.ppermute(part_late, SECTION, onward)
    direct = lax.ppermute(part_direct, SECTION, [(1, 0), (2, 7), (3, 6)])
    around = lax.ppermute(moved, SECTION, [(5, 6), (6, 7), (7, 0)])
    level = level.reshape(4, 2, 12, D)
    halves = [level[:, 0].reshape(48, D), level[:, 1].reshape(48, D)]
    level = jnp.where(core == 0, *halves) + lax.ppermute(
        jnp.where(core == 0, *halves[::-1]), "c", swap
    )
    level = level.reshape(4, 12, D)
    mine, direct, around, level = lax.optimization_barrier((mine, direct, around, level))
    other = [
        lax.ppermute(part, "c", swap) for part in jnp.split(mine, SWAPS, axis=0)
    ]

    times = time_rows(timestep).astype(jnp.float32).reshape(-1, 1, D)
    stream_out = run_block(place, times, gain_row, mine, other, early, late, direct, around)

    pieces = lax.all_to_all(level, "yl", 0, 0, tiled=True)
    stream_out, pieces = lax.optimization_barrier((stream_out, pieces))
    weight_grad = jnp.sum(pieces.reshape(4, 12, D), axis=0)
    return (stream_out[None], weight_grad[None])


def solution(mesh):
    fine = Mesh(mesh.devices.reshape(4, 2, 8, 4, 2), AXES)
    section, dp = ("x", "yh"), ("z", "yl", "c")
    return jax.shard_map(
        on_device,
        mesh=fine,
        in_specs=(
            P(section, dp, None),
            P(dp),
            P(section, None),
            P(section, dp, None),
            P(section, dp, None),
            P(None, dp, None),
            P(section, dp, None),
            P(section, dp, None),
        ),
        out_specs=(P(section, dp, None), P(section, dp, None)),
        check_vma=False,
    )
```

```python
import math

import jax
import jax.numpy as jnp
import numpy as np
from jax import lax
from jax.experimental import pallas as pl
from jax.experimental.pallas import tpu as pltpu
from jax.sharding import Mesh
from jax.sharding import PartitionSpec as P

D = 768
HEADS = 12
HEAD_DIM = 64
SEQ = 257
PAD = 272
KEYS = 384
HALF = D // 2
EARLY = 176
DIRECT = 384
SWAPS = 4
SECTIONS = 8
REPLICAS = 64
AXES = ("x", "yh", "z", "yl", "c")
SECTION = ("x", "yh")


def time_rows(timestep):
    half_width = D // 2
    frequency = jnp.exp(
        -math.log(10000.0) * jnp.arange(half_width).astype(jnp.float32) / half_width
    )
    angles = timestep.astype(jnp.float32)[:, None] * frequency[None, :]
    return jnp.concatenate([jnp.cos(angles), jnp.sin(angles)], axis=1).astype(jnp.bfloat16)


GROUPS = ((384, 192), (0, 288), (288, 96))


def weight_copies(mine, other, held, sems):
    copies = []
    for group, (start, count) in enumerate(GROUPS):
        rows = pl.ds(start, count)
        pairs = [(mine.at[:, rows], held.at[0, :, rows])]
        for i, ref in enumerate(other):
            deep = ref.shape[0]
            pairs.append((ref.at[:, rows], held.at[1, pl.ds(deep * i, deep), rows]))
        copies.append(
            [
                pltpu.make_async_copy(source, target, sems.at[group * len(pairs) + i])
                for i, (source, target) in enumerate(pairs)
            ]
        )
    return copies


def gathered(held, start, count):
    return jnp.concatenate(
        [held[half, :, start : start + count, :].reshape(-1, HALF) for half in range(2)], axis=1
    )


def block_kernel(place_ref, time_ref, gain_ref, mine, *refs):
    other, refs = refs[:SWAPS], refs[SWAPS:]
    early, late, direct, around, out_ref, *refs = refs
    held, entering, skip, block_in, normed, qkv_rows, image_context, context, *refs = refs
    scores_ref, powered_ref, sems = refs
    join_copies, qkv_copies, out_copies = weight_copies(mine, other, held, sems)
    for copy in join_copies + qkv_copies + out_copies:
        copy.start()
    count = out_ref.shape[0]
    images = count // SEQ
    section = place_ref[1]
    decoder = (section == 0) | (section >= 5)
    first_half = pl.multiple_of(place_ref[0] * HALF, 128)
    second_half = pl.multiple_of(HALF - place_ref[0] * HALF, 128)
    natural = ((first_half, 0), (second_half, HALF))
    for image in range(images):
        qkv_rows[image, 256:] = jnp.zeros((KEYS - 256, 3 * D), jnp.bfloat16)

    for copy in join_copies:
        copy.wait()

    @pl.when(decoder)
    def _():
        entering[:EARLY] = early[...]
        entering[EARLY:] = late[...]

        @pl.when(section == 5)
        def _():
            skip[...] = entering[...]

        @pl.when(section != 5)
        def _():
            skip[:DIRECT] = direct[...]
            skip[DIRECT:] = around[...]

        join = gathered(held, 4 * 96, 192)
        mixed = jnp.dot(entering[...], join[:D], preferred_element_type=jnp.float32)
        mixed = mixed + jnp.dot(skip[...], join[D:], preferred_element_type=jnp.float32)
        for here, start in natural:
            block_in[:count, pl.ds(here, HALF)] = mixed[:, start : start + HALF].astype(
                jnp.bfloat16
            )

    @pl.when(jnp.logical_not(decoder))
    def _():
        block_in[:EARLY] = early[...]
        block_in[EARLY:count] = late[...]

        @pl.when(section == 1)
        def _():
            for image in range(images):
                block_in[SEQ * image : SEQ * image + 1] = time_ref[image].astype(jnp.bfloat16)

    @pl.loop(0, block_in.shape[0] // 112)
    def _(part):
        rows = pl.ds(pl.multiple_of(part * 112, 16), 112)
        floats = block_in[rows].astype(jnp.float32)
        center = jnp.mean(floats, axis=-1, keepdims=True)
        moved = floats - center
        spread = jnp.mean(jnp.square(moved), axis=-1, keepdims=True)
        normed[rows] = (moved * lax.rsqrt(spread + 1e-05) * gain_ref[...]).astype(jnp.bfloat16)

    for copy in qkv_copies:
        copy.wait()
    for part in range(3):
        columns = slice(D * part, D * part + D)
        product = jnp.dot(
            normed[:count],
            gathered(held, 96 * part, 96),
            preferred_element_type=jnp.float32,
        ).astype(jnp.bfloat16)
        for image in range(images):
            qkv_rows[image, :SEQ, columns] = product[SEQ * image : SEQ * image + SEQ]

    @pl.loop(0, images)
    def _(image):
        low_q = lax.broadcasted_iota(jnp.int32, (PAD, 128), 1) < HEAD_DIM
        low_k = lax.broadcasted_iota(jnp.int32, (KEYS, 128), 1) < HEAD_DIM
        real = lax.broadcasted_iota(jnp.int32, (PAD, 128), 1) == 0
        zero = jnp.zeros((), jnp.bfloat16)
        one = jnp.ones((), jnp.bfloat16)
        for pair in range(HEADS // 2):
            lanes = 128 * pair
            queries = qkv_rows[image, :PAD, lanes : lanes + 128]
            keys = qkv_rows[image, :, D + lanes : D + lanes + 128]
            values = qkv_rows[image, :, 2 * D + lanes : 2 * D + lanes + 128]
            sums = []
            for low in (True, False):
                here_q = low_q if low else jnp.logical_not(low_q)
                here_k = low_k if low else jnp.logical_not(low_k)
                scores = lax.dot_general(
                    jnp.where(here_q, queries, zero),
                    keys,
                    (((1,), (1,)), ((), ())),
                    preferred_element_type=jnp.float32,
                )
                factor = HEAD_DIM ** (-0.5) * math.log2(math.e)
                scores_ref[...] = scores
                for first, size in ((0, 128), (128, 128), (256, 16)):
                    rows = slice(first, first + size)
                    main = scores_ref[rows, :256]
                    last = jnp.where(real[:size], scores_ref[rows, 256:], -1e30)
                    widest = jnp.maximum(jnp.maximum(main[:, :128], main[:, 128:]), last)
                    row_max = jnp.max(widest, axis=-1, keepdims=True)
                    powered_ref[rows, :256] = jnp.exp2((main - row_max) * factor).astype(jnp.bfloat16)
                    powered_ref[rows, 256:] = jnp.exp2((last - row_max) * factor).astype(jnp.bfloat16)
                powered = powered_ref[...]
                sums.append(
                    jnp.dot(powered, jnp.where(here_k, values, one), preferred_element_type=jnp.float32)
                )
            own = jnp.where(low_q, sums[0], sums[1])
            total = pltpu.roll(jnp.where(low_q, sums[1], sums[0]), HEAD_DIM, 1)
            here, start = natural[pair // 3]
            column = pl.multiple_of(here + (lanes - start), 128)
            image_context[image, :, pl.ds(column, 128)] = (own / total).astype(jnp.bfloat16)

    for image in range(images):
        context[SEQ * image : SEQ * image + SEQ] = image_context[image, :SEQ]
    for copy in out_copies:
        copy.wait()
    projected = jnp.dot(
        context[...], gathered(held, 3 * 96, 96), preferred_element_type=jnp.float32
    )
    for here, start in natural:
        columns = pl.ds(here, HALF)
        out_ref[:, columns] = (
            block_in[:count, columns].astype(jnp.float32) + projected[:, start : start + HALF]
        ).astype(jnp.bfloat16)


def run_block(place, times, gain_row, mine, other, early, late, direct, around):
    whole = pl.BlockSpec(memory_space=pltpu.VMEM)
    rows = early.shape[0] + late.shape[0]
    images = rows // SEQ
    return pl.pallas_call(
        block_kernel,
        out_shape=jax.ShapeDtypeStruct((rows, D), jnp.bfloat16),
        in_specs=[pl.BlockSpec(memory_space=pltpu.SMEM)]
        + [whole] * 2
        + [pl.BlockSpec(memory_space=pl.ANY)] * (1 + SWAPS)
        + [whole] * 4,
        out_specs=whole,
        scratch_shapes=[
            pltpu.VMEM((2, *mine.shape), jnp.bfloat16),
            pltpu.VMEM((rows, D), jnp.bfloat16),
            pltpu.VMEM((rows, D), jnp.bfloat16),
            pltpu.VMEM((pl.cdiv(rows, 112) * 112, D), jnp.bfloat16),
            pltpu.VMEM((pl.cdiv(rows, 112) * 112, D), jnp.bfloat16),
            pltpu.VMEM((images, KEYS, 3 * D), jnp.bfloat16),
            pltpu.VMEM((images, PAD, D), jnp.bfloat16),
            pltpu.VMEM((rows, D), jnp.bfloat16),
            pltpu.VMEM((PAD, KEYS), jnp.float32),
            pltpu.VMEM((PAD, KEYS), jnp.bfloat16),
            pltpu.SemaphoreType.DMA((len(GROUPS) * (1 + SWAPS),)),
        ],
        compiler_params=pltpu.CompilerParams(vmem_limit_bytes=57 * 2**20),
        cost_estimate=pl.CostEstimate(
            flops=images * 2 * SEQ * D * D * 7, bytes_accessed=12 * 2**20, transcendentals=0
        ),
    )(place, times, gain_row, mine, *other, early, late, direct, around)


def arrival_places(core):
    slot = np.arange(576)
    deep = slot >= 384
    row = np.where(deep, slot - 384, slot % 96)
    depth = np.where(deep, 24, 12)
    arrival = (row // depth) % 2 ^ core
    packed = np.where(deep, 48, slot // 96 * 12) + row % depth
    return ((row // (2 * depth) * 2 + arrival) * 72 + packed).astype(np.int32)


def on_device(
    stream_in, timestep, ln_gain, qkv_weight, out_weight, join_weight, ctx_saved, out_cot
):
    section = lax.axis_index(SECTION)
    core = lax.axis_index("c")
    y_low = lax.axis_index("yl")
    place = jnp.stack([core, section]).astype(jnp.int32)
    onward = [(s, (s + 1) % SECTIONS) for s in range(SECTIONS)]
    swap = [(0, 1), (1, 0)]

    term = lax.dot_general(
        ctx_saved[0], out_cot[0], (((0,), (0,)), ((), ())), preferred_element_type=jnp.float32
    )
    level = lax.psum_scatter(term, "z", scatter_dimension=0, tiled=True)

    join_rows = lax.dynamic_index_in_dim(
        join_weight, jnp.clip(section - 4, 0, 3), 0, keepdims=False
    )

    high = lax.reduce_precision(ln_gain, 8, 7)
    middle = lax.reduce_precision(ln_gain - high, 8, 7)
    gain_parts = jnp.concatenate([high, middle, ln_gain - high - middle], axis=0).astype(
        jnp.bfloat16
    )

    def pack(half, gain_half):
        columns = HALF * half
        qkv = lax.dynamic_slice_in_dim(qkv_weight[0].reshape(12, 3, D), columns, HALF, 2)
        return jnp.concatenate(
            [
                qkv.transpose(1, 0, 2).reshape(36, HALF),
                lax.dynamic_slice_in_dim(out_weight[0], columns, HALF, 1),
                lax.dynamic_slice_in_dim(join_rows, columns, HALF, 1),
                lax.dynamic_slice_in_dim(gain_parts, HALF * gain_half, HALF, 1),
            ],
            axis=0,
        )

    own_pack, cross_pack, whole = lax.optimization_barrier(
        (pack(core, core), pack(1 - core, core), stream_in[0])
    )
    straight = lax.ppermute(own_pack, SECTION, onward)
    crossed = lax.ppermute(
        cross_pack,
        AXES,
        [
            (i, ((i // REPLICAS + 1) % SECTIONS) * REPLICAS + ((i % REPLICAS) ^ 1))
            for i in range(SECTIONS * REPLICAS)
        ],
    )
    gain_halves = [
        jnp.sum(part[72:].astype(jnp.float32), axis=0, keepdims=True) for part in (straight, crossed)
    ]
    gain_row = jnp.where(
        core == 0,
        jnp.concatenate(gain_halves, axis=1),
        jnp.concatenate(gain_halves[::-1], axis=1),
    )
    pair = jnp.concatenate([straight[:72], crossed[:72]], axis=0)
    places = jnp.where(core == 0, arrival_places(0), arrival_places(1))
    source = lax.broadcasted_iota(jnp.int32, (576, 576), 1)
    order = (source == places[:, None]).astype(jnp.bfloat16)
    order, pair = lax.optimization_barrier((order, pair))
    near = lax.all_gather(pair, "yl", axis=0, tiled=True)
    near = jnp.dot(
        order, near, preferred_element_type=jnp.float32
    ).astype(jnp.bfloat16)

    early = lax.ppermute(whole[:EARLY], SECTION, onward)
    moved = lax.ppermute(whole[DIRECT:], SECTION, [(1, 7), (2, 6), (3, 5)])

    near, part_direct, part_late, gain_row, moved, early = lax.optimization_barrier(
        (near, whole[:DIRECT], whole[EARLY:], gain_row, moved, early)
    )
    mine = lax.all_gather(near, "z", axis=0, tiled=False)
    late = lax.ppermute(part_late, SECTION, onward)
    direct = lax.ppermute(part_direct, SECTION, [(1, 0), (2, 7), (3, 6)])
    around = lax.ppermute(moved, SECTION, [(5, 6), (6, 7), (7, 0)])
    level = level.reshape(4, 2, 12, D)
    halves = [level[:, 0].reshape(48, D), level[:, 1].reshape(48, D)]
    level = jnp.where(core == 0, *halves) + lax.ppermute(
        jnp.where(core == 0, *halves[::-1]), "c", swap
    )
    level = level.reshape(4, 12, D)
    mine, direct, around, level = lax.optimization_barrier((mine, direct, around, level))
    other = [
        lax.ppermute(part, "c", swap) for part in jnp.split(mine, SWAPS, axis=0)
    ]

    times = time_rows(timestep).astype(jnp.float32).reshape(-1, 1, D)
    stream_out = run_block(place, times, gain_row, mine, other, early, late, direct, around)

    pieces = lax.all_to_all(level, "yl", 0, 0, tiled=True)
    stream_out, pieces = lax.optimization_barrier((stream_out, pieces))
    weight_grad = jnp.sum(pieces.reshape(4, 12, D), axis=0)
    return (stream_out[None], weight_grad[None])


def solution(mesh):
    fine = Mesh(mesh.devices.reshape(4, 2, 8, 4, 2), AXES)
    section, dp = ("x", "yh"), ("z", "yl", "c")
    return jax.shard_map(
        on_device,
        mesh=fine,
        in_specs=(
            P(section, dp, None),
            P(dp),
            P(section, None),
            P(section, dp, None),
            P(section, dp, None),
            P(None, dp, None),
            P(section, dp, None),
            P(section, dp, None),
        ),
        out_specs=(P(section, dp, None), P(section, dp, None)),
        check_vma=False,
    )
```
